32 devices in a mesh: pipe: 4 (over y, core), tp: 8 (over z, x).
Axes of the slice: x: 2, y: 2, z: 4, core: 2. Of those that a mesh axis runs over, the one named last changes fastest.
Arguments:
- grad_next: bfloat16 [4, 2048, 8192], P('pipe', None, 'tp'), may hold values from -6 to 6
- inputs: bfloat16 [4, 2048, 8192], P('pipe', None, 'tp'), may hold values from -6 to 6
- dt_raw: bfloat16 [4, 2048, 128], P('pipe', None, 'tp'), may hold values from -5 to 5
- b_proj: bfloat16 [4, 2048, 1024], P('pipe', None, 'tp'), may hold values from -0.375 to 0.375
- c_proj: bfloat16 [4, 2048, 1024], P('pipe', None, 'tp'), may hold values from -0.375 to 0.375
- a_log: float32 [4, 128], P('pipe', 'tp'), may hold values from -7 to -3
- dt_bias: float32 [4, 128], P('pipe', 'tp'), may hold values from -2 to 0.5
- skip_gain: float32 [4, 128], P('pipe', 'tp'), may hold values from 0.5 to 1.5
Outputs:
- grad_inputs: bfloat16 [4, 2048, 8192], P('pipe', None, 'tp')
- grad_dt: bfloat16 [4, 2048, 128], P('pipe', None, 'tp')
The draws below stay inside these ranges and needn't reach their ends.
All inputs are finite; a program needn't handle non-finite values.
Results may differ from the reference program's by a relative error of at most 0.001.
Values may be sent and summed in bfloat16 or wider, within the bound.
A program may use at most 192 MiB of HBM per device.

```python
import jax
import jax.numpy as jnp
from jax import lax

H = 128
P_SIZE = 64
N = 256
G = 4
SPAN = 256
SEQ = 2048
SECTIONS = 4


def shard_levels(key, extent, cuts, least, high):
    factor_of, own = 1.0, jax.random.fold_in(key, 6)
    for position, parts in cuts:
        steps = jnp.exp(jax.random.uniform(jax.random.fold_in(own, position), (parts,), jnp.float32, least / len(cuts), high / len(cuts)))
        factor_of = factor_of * jnp.repeat(steps, extent[position] // parts).reshape([-1 if axis == position else 1 for axis in range(len(extent))])
    return factor_of


def centred(stream_key, extent, deviation, most, split=(), kind=jnp.bfloat16):
    values = deviation * jax.random.normal(stream_key, extent, jnp.float32)
    if split:
        values = values * shard_levels(stream_key, extent, split, -0.22, 0.18)
    return jnp.clip(values, -most, most).astype(kind)


def setup_inputs(seed: int = 0) -> dict:
    seeds = jax.random.split(jax.random.key(seed), 9)
    grad_next = centred(seeds[0], (SECTIONS, SEQ, H * P_SIZE), 1.0, 6.0, ((0, 4), (2, 8)))
    inputs = centred(seeds[1], (SECTIONS, SEQ, H * P_SIZE), 1.0, 6.0, ((0, 4), (2, 8)))
    dt_raw = centred(seeds[2], (SECTIONS, SEQ, H), 1.0, 5.0, ((0, 4), (2, 8)))
    b_proj = centred(seeds[3], (SECTIONS, SEQ, G * N), (1.0 / N ** 0.5), 0.375, ((0, 4), (2, 8)))
    c_proj = centred(seeds[4], (SECTIONS, SEQ, G * N), (1.0 / N ** 0.5), 0.375, ((0, 4), (2, 8)))
    a_log = jnp.clip(-7.0 + 4.0 * jax.random.uniform(seeds[5], (SECTIONS, H), jnp.float32) ** shard_levels(seeds[5], (SECTIONS, H), ((0, 4), (1, 8)), -0.2, 0.2), -7.0, -3.0)
    dt_bias = jnp.clip(-2.0 + 2.5 * jax.random.uniform(seeds[6], (SECTIONS, H), jnp.float32) ** shard_levels(seeds[6], (SECTIONS, H), ((0, 4), (1, 8)), -0.2, 0.2), -2.0, 0.5)
    skip_gain = jnp.clip(0.5 + 1.0 * jax.random.uniform(seeds[7], (SECTIONS, H), jnp.float32) ** shard_levels(seeds[7], (SECTIONS, H), ((0, 4), (1, 8)), -0.2, 0.2), 0.5, 1.5)
    return dict(grad_next=grad_next, inputs=inputs, dt_raw=dt_raw, b_proj=b_proj, c_proj=c_proj, a_log=a_log, dt_bias=dt_bias, skip_gain=skip_gain)


def ssd_group(values, dt_in, a_log, bias, skip, b_rows, c_rows):
    highest = lax.Precision.HIGHEST
    length, head_count, head_width = values.shape
    block_count = length // SPAN
    step_size = jax.nn.softplus(dt_in + bias[None, :])
    log_decay = (-jnp.exp(a_log)[None, :] * step_size).reshape(block_count, SPAN, head_count)
    cumulative = jnp.cumsum(log_decay, axis=1)
    scaled_x = (values * step_size[:, :, None]).reshape(block_count, SPAN, head_count, head_width)
    b_blocks = b_rows.reshape(block_count, SPAN, b_rows.shape[1])
    c_blocks = c_rows.reshape(block_count, SPAN, c_rows.shape[1])
    scores = jnp.einsum('kin,kjn->kij', c_blocks, b_blocks, precision=highest)
    spread = cumulative[:, :, None, :] - cumulative[:, None, :, :]
    causal = (jnp.arange(SPAN)[:, None] >= jnp.arange(SPAN)[None, :])[None, :, :, None]
    within = jnp.exp(jnp.where(causal, spread, -1e+30))
    weights = scores[:, :, :, None] * within
    inner = jnp.einsum('kijh,kjhp->kihp', weights, scaled_x, precision=highest)
    to_end = jnp.exp(cumulative[:, -1:, :] - cumulative)
    states = jnp.einsum('kjhp,kjn->khpn', scaled_x * to_end[:, :, :, None], b_blocks, precision=highest)
    whole_block = jnp.exp(cumulative[:, -1, :])

    def advance(state_in, packed):
        block_state, block_decay = packed
        return (block_decay[:, None, None] * state_in + block_state, state_in)
    start = jnp.zeros((head_count, head_width, b_rows.shape[1]), values.dtype)
    _, entering = lax.scan(advance, start, (states, whole_block))
    outer = jnp.einsum('kin,khpn->kihp', c_blocks, entering, precision=highest)
    outer = outer * jnp.exp(cumulative)[:, :, :, None]
    output = (inner + outer).reshape(length, head_count, head_width)
    return output + skip[None, :, None] * values

def ssd_grads(values, dt_in, a_log, bias, skip, b_rows, c_rows, cotangent):

    def forward(value_arg, dt_arg):
        return ssd_group(value_arg, dt_arg, a_log, bias, skip, b_rows, c_rows)
    _, pullback = jax.vjp(forward, values, dt_in)
    return pullback(cotangent)

def reference(grad_next, inputs, dt_raw, b_proj, c_proj, a_log, dt_bias, skip_gain):
    incoming = jnp.roll(grad_next, -1, axis=0)
    per_group = H // G

    def one_section(packed):
        cot_section, in_section, dt_section, b_section, c_section, alog_section, bias_section, skip_section = packed
        length = in_section.shape[0]
        values = in_section.astype(jnp.float32).reshape(length, G, per_group, P_SIZE)
        cotangent = cot_section.astype(jnp.float32).reshape(length, G, per_group, P_SIZE)
        dt_values = dt_section.astype(jnp.float32).reshape(length, G, per_group)
        b_rows = jnp.transpose(b_section.astype(jnp.float32).reshape(length, N, G), (0, 2, 1))
        c_rows = jnp.transpose(c_section.astype(jnp.float32).reshape(length, N, G), (0, 2, 1))
        grads = jax.vmap(ssd_grads, in_axes=(1, 1, 0, 0, 0, 1, 1, 1), out_axes=(1, 1))(values, dt_values, alog_section.reshape(G, per_group), bias_section.reshape(G, per_group), skip_section.reshape(G, per_group), b_rows, c_rows, cotangent)
        grad_x = grads[0].reshape(length, H * P_SIZE).astype(jnp.bfloat16)
        grad_step = grads[1].reshape(length, H).astype(jnp.bfloat16)
        return (grad_x, grad_step)
    return lax.map(one_section, (incoming, inputs, dt_raw, b_proj, c_proj, a_log, dt_bias, skip_gain))
```

```python
import functools

import jax
import jax.numpy as jnp
from jax import lax
from jax.experimental import pallas as pl
from jax.experimental.pallas import tpu as pltpu
from jax.sharding import PartitionSpec as P

P_SIZE = 64
N = 256
G = 4
SPAN = 256
COPIES = 3
CHUNKS = 4
F32, BF16 = jnp.float32, jnp.bfloat16


def dot(a, b):
    return jnp.dot(a, b, preferred_element_type=F32)


def split2(v):
    hi = v.astype(BF16)
    return hi, (v - hi.astype(F32)).astype(BF16)


def split3(v):
    hi = v.astype(BF16)
    rest = v - hi.astype(F32)
    mid = rest.astype(BF16)
    return hi, mid, (rest - mid.astype(F32)).astype(BF16)


def triangle(lower):
    row = lax.broadcasted_iota(jnp.int32, (SPAN, SPAN), 0)
    col = lax.broadcasted_iota(jnp.int32, (SPAN, SPAN), 1)
    return row >= col if lower else row <= col


def running(mask, v):
    ones = jnp.where(mask, 1.0, 0.0).astype(BF16)
    hi, mid, lo = split3(v)
    return dot(ones, hi) + dot(ones, mid) + dot(ones, lo)


def widen(v, onehot):
    hi, mid, lo = split3(v)
    part = lax.broadcasted_iota(jnp.int32, v.shape, 1) // (v.shape[1] // COPIES)
    parts = jnp.where(part == 0, hi.astype(F32), jnp.where(part == 1, mid.astype(F32), lo.astype(F32)))
    return dot(parts.astype(BF16), onehot)


def head_sum(v, onehot_t):
    hi, lo = split2(v)
    return dot(hi, onehot_t) + dot(lo, onehot_t)


def steps(raw, bias, rate):
    shifted_raw = raw.astype(F32) + bias
    near = jnp.exp(-jnp.abs(shifted_raw))
    step = jnp.maximum(shifted_raw, 0.0) + jnp.log1p(near)
    slope = jnp.where(shifted_raw >= 0, 1.0, near) / (1.0 + near)
    cum = running(triangle(True), rate * step)
    middle = 0.5 * cum[SPAN - 1 :, :]
    return step, slope, jnp.exp(cum - middle), jnp.exp(middle - cum), jnp.exp(middle)


def forward_kernel(raw, bias, rate, bt, ct, x, onehot, ybar, state):
    @pl.when(pl.program_id(0) == 0)
    def _():
        state[...] = jnp.zeros_like(state)

    step, _, _, fall, half = steps(raw[...], bias[...], rate[...])
    half_row = widen(jnp.broadcast_to(half, (8, half.shape[1])), onehot[...])[0:1]
    x_hi, x_lo = split2(x[...].astype(F32) * widen(step * fall, onehot[...]))
    c_rows = ct[...].T
    s_hi, s_lo = split2(jnp.where(triangle(True), dot(c_rows, bt[...]), 0.0))
    held = half_row * state[...]
    t_hi, t_lo = split2(held)
    ybar[...] = dot(s_hi, x_hi) + dot(s_hi, x_lo) + dot(s_lo, x_hi) + dot(c_rows, t_hi) + dot(c_rows, t_lo)
    state[...] = half_row * (held + dot(bt[...], x_hi) + dot(bt[...], x_lo))


def backward_kernel(
    raw, bias, rate, bt, ct, x, g, ybar, onehot, onehot_t, skip, state_in, carry_in, *rest
):
    grad_x, grad_dt, state, carry = rest[-4:]

    @pl.when(pl.program_id(0) == 0)
    def _():
        state[...] = state_in[...]
        carry[...] = carry_in[...]

    step, slope, rise, fall, _ = steps(raw[...], bias[...], rate[...])
    wide_rise = widen(rise, onehot[...])
    half_row = wide_rise[SPAN - 1 :, :]
    grad = g[...].astype(F32)
    g_hi, g_lo = split2(grad * wide_rise)
    b_rows = bt[...].T
    s_hi, s_lo = split2(jnp.where(triangle(False), dot(b_rows, ct[...]), 0.0))
    held = half_row * state[...]
    t_hi, t_lo = split2(held)
    zbar = dot(s_hi, g_hi) + dot(s_hi, g_lo) + dot(s_lo, g_hi) + dot(b_rows, t_hi) + dot(b_rows, t_lo)
    state[...] = half_row * (held + dot(ct[...], g_hi) + dot(ct[...], g_lo))
    grad_x[...] = (widen(step * fall, onehot[...]) * zbar + skip[...] * grad).astype(BF16)
    by_x = fall * head_sum(x[...].astype(F32) * zbar, onehot_t[...])
    by_y = rise * head_sum(grad * ybar[...], onehot_t[...])
    decay = running(triangle(False), by_y - step * by_x) + carry[0:1, :]
    carry[...] = jnp.broadcast_to(decay[0:1, :], carry.shape)
    heads = grad_dt.shape[1]
    grad_dt[...] = (slope * (by_x + rate[...] * decay))[:, :heads].astype(BF16)


def shifted(value, axis, by):
    length = lax.axis_size(axis)
    return lax.ppermute(value, axis, [(i, (i + by) % length) for i in range(length)])


def gather_rows(b_proj, c_proj):
    length, columns = b_proj.shape
    ways = lax.axis_size("tp")
    per_group = ways // G
    width = columns // G
    order = (jnp.arange(columns)[:, None] % width) * G + jnp.arange(columns)[:, None] // width
    pick = (order == jnp.arange(columns)[None, :]).astype(BF16)

    def turned(rows):
        return lax.dot_general(pick, rows, (((1,), (1,)), ((), ())), preferred_element_type=F32).astype(BF16)

    both = jnp.stack([turned(b_proj).reshape(G, width, length), turned(c_proj).reshape(G, width, length)], axis=1)
    strided = [[g * per_group + r for g in range(G)] for r in range(per_group)]
    mine = lax.all_to_all(both, "tp", 0, 0, axis_index_groups=strided, tiled=True)
    if per_group > 1:
        close = [[g * per_group + r for r in range(per_group)] for g in range(G)]
        mine = lax.all_gather(mine, "tp", axis=0, axis_index_groups=close, tiled=True)
    return mine[:, 0].reshape(N, length), mine[:, 1].reshape(N, length)


def body(grad_next, inputs, dt_raw, b_proj, c_proj, a_log, dt_bias, skip_gain):
    length, width = inputs.shape[1:]
    heads = a_log.shape[1]
    blocks = length // SPAN
    chunks = min(CHUNKS, blocks)
    per_chunk = blocks // chunks
    rows = length // chunks
    arriving = [shifted(grad_next[0, k * rows : (k + 1) * rows], "pipe", -1) for k in range(chunks - 1, -1, -1)]
    bt, ct = gather_rows(b_proj[0], c_proj[0])
    raw = jnp.tile(dt_raw[0], (1, COPIES))
    bias = jnp.tile(dt_bias, (1, COPIES))
    rate = -jnp.exp(jnp.tile(a_log, (1, COPIES)))
    skip = jnp.repeat(skip_gain, P_SIZE, axis=1)
    lanes = heads * COPIES
    onehot = (jnp.arange(lanes)[:, None] % heads == jnp.arange(width)[None, :] // P_SIZE).astype(BF16)
    onehot_t = (jnp.arange(lanes)[None, :] % heads == jnp.arange(width)[:, None] // P_SIZE).astype(BF16)
    x = inputs[0]

    def whole(shape):
        return pl.BlockSpec(shape, lambda k: (0, 0))

    def token_rows(columns, at):
        return pl.BlockSpec((SPAN, columns), lambda k: (at(k), 0))

    def token_cols(at):
        return pl.BlockSpec((N, SPAN), lambda k: (0, at(k)))

    params = pltpu.CompilerParams(vmem_limit_bytes=56 * 1024 * 1024, dimension_semantics=("arbitrary",))
    same = lambda k: k
    ybar = pl.pallas_call(
        forward_kernel,
        grid=(blocks,),
        in_specs=[
            token_rows(lanes, same),
            whole((1, lanes)),
            whole((1, lanes)),
            token_cols(same),
            token_cols(same),
            token_rows(width, same),
            whole((lanes, width)),
        ],
        out_specs=token_rows(width, same),
        out_shape=jax.ShapeDtypeStruct((length, width), F32),
        scratch_shapes=[pltpu.VMEM((N, width), F32)],
        compiler_params=params,
        cost_estimate=pl.CostEstimate(flops=18 * length * N * width, bytes_accessed=8 * length * width, transcendentals=0),
        name="states_forward",
    )(raw, bias, rate, bt, ct, x, onehot)

    state = jnp.zeros((N, width), F32)
    carry = jnp.zeros((8, lanes), F32)
    grads = ()
    for index, g in enumerate(arriving):
        base = (chunks - 1 - index) * per_chunk
        at = lambda k, base=base: base + per_chunk - 1 - k
        local = lambda k: per_chunk - 1 - k
        fixed = 13
        grad_x, grad_dt, state, carry = pl.pallas_call(
            backward_kernel,
            grid=(per_chunk,),
            in_specs=[
                token_rows(lanes, at),
                whole((1, lanes)),
                whole((1, lanes)),
                token_cols(at),
                token_cols(at),
                token_rows(width, at),
                token_rows(width, local),
                token_rows(width, at),
                whole((lanes, width)),
                whole((width, lanes)),
                whole((1, width)),
                whole((N, width)),
                whole((8, lanes)),
            ]
            + [pl.BlockSpec(memory_space=pl.ANY)] * len(grads),
            out_specs=[
                token_rows(width, at),
                token_rows(heads, at),
                whole((N, width)),
                whole((8, lanes)),
            ],
            out_shape=[
                jax.ShapeDtypeStruct((length, width), BF16),
                jax.ShapeDtypeStruct((length, heads), BF16),
                jax.ShapeDtypeStruct((N, width), F32),
                jax.ShapeDtypeStruct((8, lanes), F32),
            ],
            input_output_aliases={fixed: 0, fixed + 1: 1} if grads else {},
            compiler_params=params,
            cost_estimate=pl.CostEstimate(flops=30 * rows * N * width, bytes_accessed=12 * rows * width, transcendentals=0),
            name="gradients_%d" % index,
        )(raw, bias, rate, bt, ct, x, g, ybar, onehot, onehot_t, skip, state, carry, *grads)
        grads = (grad_x, grad_dt)
    return grads[0][None], grads[1][None]


def solution(mesh):
    wide, narrow = P("pipe", None, "tp"), P("pipe", "tp")
    return jax.shard_map(
        body,
        mesh=mesh,
        in_specs=(wide, wide, wide, wide, wide, narrow, narrow, narrow),
        out_specs=(wide, wide),
        check_vma=False,
    )
```

```python
import functools

import functools

import jax
import jax.numpy as jnp
from jax import lax
from jax.experimental import pallas as pl
from jax.experimental.pallas import tpu as pltpu
from jax.sharding import PartitionSpec as P

P_SIZE = 64
N = 256
G = 4
SPAN = 256
COPIES = 3
CHUNKS = 4
F32, BF16 = jnp.float32, jnp.bfloat16


def dot(a, b):
    return jnp.dot(a, b, preferred_element_type=F32)


def split2(v):
    hi = v.astype(BF16)
    return hi, (v - hi.astype(F32)).astype(BF16)


def split3(v):
    hi = v.astype(BF16)
    rest = v - hi.astype(F32)
    mid = rest.astype(BF16)
    return hi, mid, (rest - mid.astype(F32)).astype(BF16)


def triangle(lower):
    row = lax.broadcasted_iota(jnp.int32, (SPAN, SPAN), 0)
    col = lax.broadcasted_iota(jnp.int32, (SPAN, SPAN), 1)
    return row >= col if lower else row <= col


def running(mask, v):
    ones = jnp.where(mask, 1.0, 0.0).astype(BF16)
    hi, mid, lo = split3(v)
    return dot(ones, hi) + dot(ones, mid) + dot(ones, lo)


def widen(v, onehot):
    hi, mid, lo = split3(v)
    part = lax.broadcasted_iota(jnp.int32, v.shape, 1) // (v.shape[1] // COPIES)
    parts = jnp.where(part == 0, hi.astype(F32), jnp.where(part == 1, mid.astype(F32), lo.astype(F32)))
    return dot(parts.astype(BF16), onehot)


def head_sum(v, onehot_t):
    hi, lo = split2(v)
    return dot(hi, onehot_t) + dot(lo, onehot_t)


def steps(raw, bias, rate):
    shifted_raw = raw.astype(F32) + bias
    near = jnp.exp(-jnp.abs(shifted_raw))
    step = jnp.maximum(shifted_raw, 0.0) + jnp.log1p(near)
    slope = jnp.where(shifted_raw >= 0, 1.0, near) / (1.0 + near)
    cum = running(triangle(True), rate * step)
    middle = 0.5 * cum[SPAN - 1 :, :]
    return step, slope, jnp.exp(cum - middle), jnp.exp(middle - cum), jnp.exp(middle)


def forward_sends(blocks, per_group, raw, bias, rate, out, x, onehot, ybar, bt, ct, state, land, send1, recv1, send2, recv2):
    now = pl.program_id(0)
    me = lax.axis_index("tp")
    group, place = me // per_group, me % per_group

    def across(j, d):
        to = (group + d) % G
        return pltpu.make_async_remote_copy(
            src_ref=out.at[j, to],
            dst_ref=land.at[j, place, group],
            send_sem=send1.at[j, d],
            recv_sem=recv1.at[j, d],
            device_id={"tp": to * per_group + place},
            device_id_type=pl.DeviceIdType.MESH,
        )

    def beside(j, d):
        return pltpu.make_async_remote_copy(
            src_ref=land.at[j, place],
            dst_ref=land.at[j, place],
            send_sem=send2.at[j, d],
            recv_sem=recv2.at[j, d],
            device_id={"tp": group * per_group + (place + d) % per_group},
            device_id_type=pl.DeviceIdType.MESH,
        )

    def own(j):
        return pltpu.make_async_copy(out.at[j, group], land.at[j, place, group], recv1.at[j, 0])

    def pass_on(j):
        own(j).wait()
        for d in range(1, G):
            across(j, d).wait_recv()
        for d in range(1, per_group):
            beside(j, d).start()

    @pl.when(now == 0)
    def _():
        barrier = pltpu.get_barrier_semaphore()
        for d in range(1, G):
            pl.semaphore_signal(
                barrier,
                inc=1,
                device_id={"tp": (group + d) % G * per_group + place},
                device_id_type=pl.DeviceIdType.MESH,
            )
        for d in range(1, per_group):
            pl.semaphore_signal(
                barrier,
                inc=1,
                device_id={"tp": group * per_group + (place + d) % per_group},
                device_id_type=pl.DeviceIdType.MESH,
            )
        pl.semaphore_wait(barrier, G - 1 + per_group - 1)

        @pl.loop(0, blocks)
        def _(j):
            own(j).start()
            for d in range(1, G):
                across(j, d).start()

        pass_on(0)

    @pl.when(now + 1 < blocks)
    def _():
        pass_on(now + 1)

    for d in range(1, per_group):
        beside(now, d).wait_recv()
    bt[...] = land[now, :, :, 0].reshape(N, SPAN)
    ct[...] = land[now, :, :, 1].reshape(N, SPAN)
    forward_kernel(raw, bias, rate, bt, ct, x, onehot, ybar, state)

    @pl.when(now == blocks - 1)
    def _():
        @pl.loop(0, blocks)
        def _(j):
            for d in range(1, G):
                across(j, d).wait_send()
            for d in range(1, per_group):
                beside(j, d).wait_send()


def forward_kernel(raw, bias, rate, bt, ct, x, onehot, ybar, state):
    @pl.when(pl.program_id(0) == 0)
    def _():
        state[...] = jnp.zeros_like(state)

    step, _, _, fall, half = steps(raw[...], bias[...], rate[...])
    half_row = widen(jnp.broadcast_to(half, (8, half.shape[1])), onehot[...])[0:1]
    x_hi, x_lo = split2(x[...].astype(F32) * widen(step * fall, onehot[...]))
    c_rows = ct[...].T
    s_hi, s_lo = split2(jnp.where(triangle(True), dot(c_rows, bt[...]), 0.0))
    held = half_row * state[...]
    t_hi, t_lo = split2(held)
    ybar[...] = dot(s_hi, x_hi) + dot(s_hi, x_lo) + dot(s_lo, x_hi) + dot(c_rows, t_hi) + dot(c_rows, t_lo)
    state[...] = half_row * (held + dot(bt[...], x_hi) + dot(bt[...], x_lo))


def backward_kernel(
    raw, bias, rate, bt, ct, x, g, ybar, onehot, onehot_t, skip, state_in, carry_in, *rest
):
    grad_x, grad_dt, state, carry = rest[-4:]

    @pl.when(pl.program_id(0) == 0)
    def _():
        state[...] = state_in[...]
        carry[...] = carry_in[...]

    step, slope, rise, fall, _ = steps(raw[...], bias[...], rate[...])
    wide_rise = widen(rise, onehot[...])
    half_row = wide_rise[SPAN - 1 :, :]
    grad = g[...].astype(F32)
    g_hi, g_lo = split2(grad * wide_rise)
    b_rows = bt[...].T
    s_hi, s_lo = split2(jnp.where(triangle(False), dot(b_rows, ct[...]), 0.0))
    held = half_row * state[...]
    t_hi, t_lo = split2(held)
    zbar = dot(s_hi, g_hi) + dot(s_hi, g_lo) + dot(s_lo, g_hi) + dot(b_rows, t_hi) + dot(b_rows, t_lo)
    state[...] = half_row * (held + dot(ct[...], g_hi) + dot(ct[...], g_lo))
    grad_x[...] = (widen(step * fall, onehot[...]) * zbar + skip[...] * grad).astype(BF16)
    by_x = fall * head_sum(x[...].astype(F32) * zbar, onehot_t[...])
    by_y = rise * head_sum(grad * ybar[...], onehot_t[...])
    decay = running(triangle(False), by_y - step * by_x) + carry[0:1, :]
    carry[...] = jnp.broadcast_to(decay[0:1, :], carry.shape)
    heads = grad_dt.shape[1]
    grad_dt[...] = (slope * (by_x + rate[...] * decay))[:, :heads].astype(BF16)


def shifted(value, axis, by):
    length = lax.axis_size(axis)
    return lax.ppermute(value, axis, [(i, (i + by) % length) for i in range(length)])


def outgoing(b_proj, c_proj):
    length, columns = b_proj.shape
    width = columns // G
    blocks = length // SPAN
    kind = jnp.arange(2 * columns) // width % 2
    entry = jnp.arange(2 * columns) // (2 * width) + jnp.arange(2 * columns) % width * G
    take = jnp.arange(columns)[None, :]
    sides = [((entry[:, None] == take) & (kind[:, None] == which)).astype(BF16) for which in range(2)]
    pick = jnp.concatenate(sides, axis=1)
    rows = jnp.concatenate([b_proj, c_proj], axis=1).reshape(blocks, SPAN, 2 * columns)
    turned = jnp.einsum("cd,ktd->kct", pick, rows, preferred_element_type=F32).astype(BF16)
    return turned.reshape(blocks, G, 2, width, SPAN)


def gather_rows(b_proj, c_proj):
    length, columns = b_proj.shape
    ways = lax.axis_size("tp")
    per_group = ways // G
    width = columns // G
    order = (jnp.arange(columns)[:, None] % width) * G + jnp.arange(columns)[:, None] // width
    pick = (order == jnp.arange(columns)[None, :]).astype(BF16)

    def turned(rows):
        return lax.dot_general(pick, rows, (((1,), (1,)), ((), ())), preferred_element_type=F32).astype(BF16)

    both = jnp.stack([turned(b_proj).reshape(G, width, length), turned(c_proj).reshape(G, width, length)], axis=1)
    strided = [[g * per_group + r for g in range(G)] for r in range(per_group)]
    mine = lax.all_to_all(both, "tp", 0, 0, axis_index_groups=strided, tiled=True)
    if per_group > 1:
        close = [[g * per_group + r for r in range(per_group)] for g in range(G)]
        mine = lax.all_gather(mine, "tp", axis=0, axis_index_groups=close, tiled=True)
    return mine[:, 0].reshape(N, length), mine[:, 1].reshape(N, length)


def body(grad_next, inputs, dt_raw, b_proj, c_proj, a_log, dt_bias, skip_gain):
    length, width = inputs.shape[1:]
    heads = a_log.shape[1]
    blocks = length // SPAN
    chunks = min(CHUNKS, blocks)
    per_chunk = blocks // chunks
    rows = length // chunks
    arriving = [shifted(grad_next[0, k * rows : (k + 1) * rows], "pipe", -1) for k in range(chunks - 1, -1, -1)]
    per_group = lax.axis_size("tp") // G
    entries = b_proj.shape[2] // G
    fused = entries % 16 == 0
    raw = jnp.tile(dt_raw[0], (1, COPIES))
    bias = jnp.tile(dt_bias, (1, COPIES))
    rate = -jnp.exp(jnp.tile(a_log, (1, COPIES)))
    skip = jnp.repeat(skip_gain, P_SIZE, axis=1)
    lanes = heads * COPIES
    onehot = (jnp.arange(lanes)[:, None] % heads == jnp.arange(width)[None, :] // P_SIZE).astype(BF16)
    onehot_t = (jnp.arange(lanes)[None, :] % heads == jnp.arange(width)[:, None] // P_SIZE).astype(BF16)
    x = inputs[0]

    def whole(shape):
        return pl.BlockSpec(shape, lambda k: (0, 0))

    def token_rows(columns, at):
        return pl.BlockSpec((SPAN, columns), lambda k: (at(k), 0))

    def token_cols(at):
        return pl.BlockSpec((N, SPAN), lambda k: (0, at(k)))

    params = pltpu.CompilerParams(vmem_limit_bytes=56 * 1024 * 1024, dimension_semantics=("arbitrary",))
    same = lambda k: k
    cost = pl.CostEstimate(flops=18 * length * N * width, bytes_accessed=8 * length * width, transcendentals=0)
    if fused:
        ybar, bt, ct = pl.pallas_call(
            functools.partial(forward_sends, blocks, per_group),
            grid=(blocks,),
            in_specs=[
                token_rows(lanes, same),
                whole((1, lanes)),
                whole((1, lanes)),
                pl.BlockSpec(memory_space=pl.ANY),
                token_rows(width, same),
                whole((lanes, width)),
            ],
            out_specs=[token_rows(width, same), token_cols(same), token_cols(same)],
            out_shape=[
                jax.ShapeDtypeStruct((length, width), F32),
                jax.ShapeDtypeStruct((N, length), BF16),
                jax.ShapeDtypeStruct((N, length), BF16),
            ],
            scratch_shapes=[
                pltpu.VMEM((N, width), F32),
                pltpu.VMEM((blocks, per_group, G, 2, entries, SPAN), BF16),
                pltpu.SemaphoreType.DMA((blocks, G)),
                pltpu.SemaphoreType.DMA((blocks, G)),
                pltpu.SemaphoreType.DMA((blocks, per_group)),
                pltpu.SemaphoreType.DMA((blocks, per_group)),
            ],
            compiler_params=pltpu.CompilerParams(
                vmem_limit_bytes=40 * 1024 * 1024,
                dimension_semantics=("arbitrary",),
                collective_id=0,
                has_side_effects=True,
            ),
            cost_estimate=cost,
            name="exchange_forward",
        )(raw, bias, rate, outgoing(b_proj[0], c_proj[0]), x, onehot)
    else:
        bt, ct = gather_rows(b_proj[0], c_proj[0])
        ybar = pl.pallas_call(
            forward_kernel,
            grid=(blocks,),
            in_specs=[
                token_rows(lanes, same),
                whole((1, lanes)),
                whole((1, lanes)),
                token_cols(same),
                token_cols(same),
                token_rows(width, same),
                whole((lanes, width)),
            ],
            out_specs=token_rows(width, same),
            out_shape=jax.ShapeDtypeStruct((length, width), F32),
            scratch_shapes=[pltpu.VMEM((N, width), F32)],
            compiler_params=params,
            cost_estimate=cost,
            name="states_forward",
        )(raw, bias, rate, bt, ct, x, onehot)

    state = jnp.zeros((N, width), F32)
    carry = jnp.zeros((8, lanes), F32)
    grads = ()
    for index, g in enumerate(arriving):
        base = (chunks - 1 - index) * per_chunk
        at = lambda k, base=base: base + per_chunk - 1 - k
        local = lambda k: per_chunk - 1 - k
        fixed = 13
        grad_x, grad_dt, state, carry = pl.pallas_call(
            backward_kernel,
            grid=(per_chunk,),
            in_specs=[
                token_rows(lanes, at),
                whole((1, lanes)),
                whole((1, lanes)),
                token_cols(at),
                token_cols(at),
                token_rows(width, at),
                token_rows(width, local),
                token_rows(width, at),
                whole((lanes, width)),
                whole((width, lanes)),
                whole((1, width)),
                whole((N, width)),
                whole((8, lanes)),
            ]
            + [pl.BlockSpec(memory_space=pl.ANY)] * len(grads),
            out_specs=[
                token_rows(width, at),
                token_rows(heads, at),
                whole((N, width)),
                whole((8, lanes)),
            ],
            out_shape=[
                jax.ShapeDtypeStruct((length, width), BF16),
                jax.ShapeDtypeStruct((length, heads), BF16),
                jax.ShapeDtypeStruct((N, width), F32),
                jax.ShapeDtypeStruct((8, lanes), F32),
            ],
            input_output_aliases={fixed: 0, fixed + 1: 1} if grads else {},
            compiler_params=params,
            cost_estimate=pl.CostEstimate(flops=30 * rows * N * width, bytes_accessed=12 * rows * width, transcendentals=0),
            name="gradients_%d" % index,
        )(raw, bias, rate, bt, ct, x, g, ybar, onehot, onehot_t, skip, state, carry, *grads)
        grads = (grad_x, grad_dt)
    return grads[0][None], grads[1][None]


def solution(mesh):
    wide, narrow = P("pipe", None, "tp"), P("pipe", "tp")
    return jax.shard_map(
        body,
        mesh=mesh,
        in_specs=(wide, wide, wide, wide, wide, narrow, narrow, narrow),
        out_specs=(wide, wide),
        check_vma=False,
    )
```

```python
import functools

import functools

import jax
import jax.numpy as jnp
import numpy as np
from jax import lax
from jax.experimental import pallas as pl
from jax.experimental.pallas import tpu as pltpu
from jax.sharding import PartitionSpec as P

P_SIZE = 64
N = 256
G = 4
SPAN = 256
COPIES = 3
F32, BF16 = jnp.float32, jnp.bfloat16


def dot(a, b):
    return jnp.dot(a, b, preferred_element_type=F32)


def split2(v):
    hi = v.astype(BF16)
    return hi, (v - hi.astype(F32)).astype(BF16)


def split3(v):
    hi = v.astype(BF16)
    rest = v - hi.astype(F32)
    mid = rest.astype(BF16)
    return hi, mid, (rest - mid.astype(F32)).astype(BF16)


def triangle(lower):
    row = lax.broadcasted_iota(jnp.int32, (SPAN, SPAN), 0)
    col = lax.broadcasted_iota(jnp.int32, (SPAN, SPAN), 1)
    return row >= col if lower else row <= col


def running(mask, v):
    ones = jnp.where(mask, 1.0, 0.0).astype(BF16)
    hi, mid, lo = split3(v)
    return dot(ones, hi) + dot(ones, mid) + dot(ones, lo)


def widen(v, onehot):
    hi, mid, lo = split3(v)
    part = lax.broadcasted_iota(jnp.int32, v.shape, 1) // (v.shape[1] // COPIES)
    parts = jnp.where(part == 0, hi.astype(F32), jnp.where(part == 1, mid.astype(F32), lo.astype(F32)))
    return dot(parts.astype(BF16), onehot)


def head_sum(v, onehot_t):
    hi, lo = split2(v)
    return dot(hi, onehot_t) + dot(lo, onehot_t)


def steps(raw, bias, rate):
    shifted_raw = raw.astype(F32) + bias
    near = jnp.exp(-jnp.abs(shifted_raw))
    step = jnp.maximum(shifted_raw, 0.0) + jnp.log1p(near)
    slope = jnp.where(shifted_raw >= 0, 1.0, near) / (1.0 + near)
    cum = running(triangle(True), rate * step)
    middle = 0.5 * cum[SPAN - 1 :, :]
    return step, slope, jnp.exp(cum - middle), jnp.exp(middle - cum), jnp.exp(middle)


def forward_sends(blocks, per_group, raw, bias, rate, out, x, onehot, ct, *rest):
    outs, (bt, state, land, send1, recv1, send2, recv2) = rest[:-7], rest[-7:]
    now = pl.program_id(0)
    me = lax.axis_index("tp")
    group, place = me // per_group, me % per_group

    def across(j, d):
        to = (group + d) % G
        return pltpu.make_async_remote_copy(
            src_ref=out.at[j, to],
            dst_ref=land.at[j, place, group],
            send_sem=send1.at[j, d],
            recv_sem=recv1.at[j, d],
            device_id={"tp": to * per_group + place},
            device_id_type=pl.DeviceIdType.MESH,
        )

    def beside(j, d):
        return pltpu.make_async_remote_copy(
            src_ref=land.at[j, place],
            dst_ref=land.at[j, place],
            send_sem=send2.at[j, d],
            recv_sem=recv2.at[j, d],
            device_id={"tp": group * per_group + (place + d) % per_group},
            device_id_type=pl.DeviceIdType.MESH,
        )

    def own(j):
        return pltpu.make_async_copy(out.at[j, group], land.at[j, place, group], recv1.at[j, 0])

    def pass_on(j):
        own(j).wait()
        for d in range(1, G):
            across(j, d).wait_recv()
        for d in range(1, per_group):
            beside(j, d).start()

    @pl.when(now == 0)
    def _():
        barrier = pltpu.get_barrier_semaphore()
        for d in range(1, G):
            pl.semaphore_signal(
                barrier,
                inc=1,
                device_id={"tp": (group + d) % G * per_group + place},
                device_id_type=pl.DeviceIdType.MESH,
            )
        for d in range(1, per_group):
            pl.semaphore_signal(
                barrier,
                inc=1,
                device_id={"tp": group * per_group + (place + d) % per_group},
                device_id_type=pl.DeviceIdType.MESH,
            )
        pl.semaphore_wait(barrier, G - 1 + per_group - 1)

        @pl.loop(0, blocks)
        def _(j):
            own(j).start()
            for d in range(1, G):
                across(j, d).start()

        pass_on(0)

    @pl.when(now + 1 < blocks)
    def _():
        pass_on(now + 1)

    for d in range(1, per_group):
        beside(now, d).wait_recv()
    bt[...] = land[now, :, :, 0].reshape(N, SPAN)
    ct[...] = land[now, :, :, 1].reshape(N, SPAN)
    forward_kernel(raw, bias, rate, bt, ct, x, onehot, *outs, state)

    @pl.when(now == blocks - 1)
    def _():
        @pl.loop(0, blocks)
        def _(j):
            for d in range(1, G):
                across(j, d).wait_send()
            for d in range(1, per_group):
                beside(j, d).wait_send()


def forward_kernel(
    raw, bias, rate, bt, ct, x, onehot, ybar, wide_rise, wide_fall, turned_hi, turned_lo, b_out, step_out, slope_out, rise_out, fall_out, state
):
    @pl.when(pl.program_id(0) == 0)
    def _():
        state[...] = jnp.zeros_like(state)

    step, slope, rise, fall, half = steps(raw[...], bias[...], rate[...])
    step_out[...], slope_out[...], rise_out[...], fall_out[...] = step, slope, rise, fall
    wide_rise[...] = widen(rise, onehot[...])
    scale = widen(step * fall, onehot[...])
    wide_fall[...] = scale
    half_row = widen(jnp.broadcast_to(half, (8, half.shape[1])), onehot[...])[0:1]
    x_hi, x_lo = split2(x[...].astype(F32) * scale)
    c_rows, b_rows = ct[...].T, bt[...].T
    b_out[...] = b_rows
    turned_hi[...], turned_lo[...] = split2(jnp.where(triangle(False), dot(b_rows, ct[...]), 0.0))
    s_hi, s_lo = split2(jnp.where(triangle(True), dot(c_rows, bt[...]), 0.0))
    held = half_row * state[...]
    t_hi, t_lo = split2(held)
    ybar[...] = dot(s_hi, x_hi) + dot(s_hi, x_lo) + dot(s_lo, x_hi) + dot(c_rows, t_hi) + dot(c_rows, t_lo)
    state[...] = half_row * (held + dot(bt[...], x_hi) + dot(bt[...], x_lo))


def backward_kernel(
    x, g, ybar, wide_rise, wide_fall, s_hi, s_lo, b_rows, ct, step, slope, rise, fall,
    rate, skip, onehot, onehot_t, grad_x, grad_dt, state, by_all, decay_all
):
    now, blocks = pl.program_id(0), pl.num_programs(0)

    @pl.when(now == 0)
    def _():
        state[...] = jnp.zeros_like(state)

    half_row = wide_rise[SPAN - 1 :, :]
    grad = g[...].astype(F32)
    g_hi, g_lo = split2(grad * wide_rise[...])
    held = half_row * state[...]
    t_hi, t_lo = split2(held)
    zbar = dot(s_hi[...], g_hi) + dot(s_hi[...], g_lo) + dot(s_lo[...], g_hi) + dot(b_rows[...], t_hi) + dot(b_rows[...], t_lo)
    state[...] = half_row * (held + dot(ct[...], g_hi) + dot(ct[...], g_lo))
    skip_row = widen(jnp.broadcast_to(skip[...], (8, skip.shape[1])), onehot[...])[0:1]
    grad_x[...] = (wide_fall[...] * zbar + skip_row * grad).astype(BF16)
    by_x = fall[...] * head_sum(x[...].astype(F32) * zbar, onehot_t[...])
    by_y = rise[...] * head_sum(grad * ybar[...], onehot_t[...])
    here = pl.ds(pl.multiple_of((blocks - 1 - now) * SPAN, SPAN), SPAN)
    by_all[here, :] = by_x
    decay_all[here, :] = by_y - step[...] * by_x

    @pl.when(now == blocks - 1)
    def _():
        length, heads = grad_dt.shape
        carry = jnp.zeros((1, by_all.shape[1]), F32)
        for j in range(length // SPAN - 1, -1, -1):
            part = slice(j * SPAN, (j + 1) * SPAN)
            decay = running(triangle(False), decay_all[part, :]) + carry
            carry = decay[0:1, :]
            grad_dt[part, :] = (slope[part, :] * (by_all[part, :] + rate[...] * decay))[:, :heads].astype(BF16)


def shifted(value, axis, by):
    length = lax.axis_size(axis)
    return lax.ppermute(value, axis, [(i, (i + by) % length) for i in range(length)])


def outgoing(b_proj, c_proj):
    length, columns = b_proj.shape
    width = columns // G
    blocks = length // SPAN
    kind = np.arange(2 * columns) // width % 2
    entry = np.arange(2 * columns) // (2 * width) + np.arange(2 * columns) % width * G
    take = np.arange(columns)[None, :]
    sides = [((entry[:, None] == take) & (kind[:, None] == which)).astype(BF16) for which in range(2)]
    pick = jnp.asarray(np.concatenate(sides, axis=1))
    rows = jnp.concatenate([b_proj, c_proj], axis=1).reshape(blocks, SPAN, 2 * columns)
    turned = jnp.einsum("cd,ktd->kct", pick, rows, preferred_element_type=F32).astype(BF16)
    return turned.reshape(blocks, G, 2, width, SPAN)


def gather_rows(b_proj, c_proj):
    length, columns = b_proj.shape
    ways = lax.axis_size("tp")
    per_group = ways // G
    width = columns // G
    order = (jnp.arange(columns)[:, None] % width) * G + jnp.arange(columns)[:, None] // width
    pick = (order == jnp.arange(columns)[None, :]).astype(BF16)

    def turned(rows):
        return lax.dot_general(pick, rows, (((1,), (1,)), ((), ())), preferred_element_type=F32).astype(BF16)

    both = jnp.stack([turned(b_proj).reshape(G, width, length), turned(c_proj).reshape(G, width, length)], axis=1)
    strided = [[g * per_group + r for g in range(G)] for r in range(per_group)]
    mine = lax.all_to_all(both, "tp", 0, 0, axis_index_groups=strided, tiled=True)
    if per_group > 1:
        close = [[g * per_group + r for r in range(per_group)] for g in range(G)]
        mine = lax.all_gather(mine, "tp", axis=0, axis_index_groups=close, tiled=True)
    return mine[:, 0].reshape(N, length), mine[:, 1].reshape(N, length)


def body(grad_next, inputs, dt_raw, b_proj, c_proj, a_log, dt_bias, skip_gain):
    length, width = inputs.shape[1:]
    heads = a_log.shape[1]
    blocks = length // SPAN
    g = shifted(grad_next[0], "pipe", -1)
    per_group = lax.axis_size("tp") // G
    entries = b_proj.shape[2] // G
    fused = entries % 16 == 0
    raw = jnp.tile(dt_raw[0], (1, COPIES))
    bias = jnp.tile(dt_bias, (1, COPIES))
    rate = -jnp.exp(jnp.tile(a_log, (1, COPIES)))
    skip = jnp.tile(skip_gain, (1, COPIES))
    lanes = heads * COPIES
    onehot = (np.arange(lanes)[:, None] % heads == np.arange(width)[None, :] // P_SIZE).astype(BF16)
    onehot_t = np.ascontiguousarray(onehot.T)
    onehot, onehot_t = jnp.asarray(onehot), jnp.asarray(onehot_t)
    x = inputs[0]

    def whole(shape):
        return pl.BlockSpec(shape, lambda k: (0, 0))

    def token_rows(columns, at):
        return pl.BlockSpec((SPAN, columns), lambda k: (at(k), 0))

    def token_cols(at):
        return pl.BlockSpec((N, SPAN), lambda k: (0, at(k)))

    params = pltpu.CompilerParams(vmem_limit_bytes=56 * 1024 * 1024, dimension_semantics=("arbitrary",))
    same = lambda k: k
    cost = pl.CostEstimate(flops=18 * length * N * width, bytes_accessed=8 * length * width, transcendentals=0)
    specs, shapes = [], []
    for columns, kind in [(width, F32)] * 3 + [(SPAN, BF16)] * 2 + [(N, BF16)] + [(lanes, F32)] * 4:
        specs.append(token_rows(columns, same))
        shapes.append(jax.ShapeDtypeStruct((length, columns), kind))
    if fused:
        ct, *kept = pl.pallas_call(
            functools.partial(forward_sends, blocks, per_group),
            grid=(blocks,),
            in_specs=[
                token_rows(lanes, same),
                whole((1, lanes)),
                whole((1, lanes)),
                pl.BlockSpec(memory_space=pl.ANY),
                token_rows(width, same),
                whole((lanes, width)),
            ],
            out_specs=[token_cols(same)] + specs,
            out_shape=[jax.ShapeDtypeStruct((N, length), BF16)] + shapes,
            scratch_shapes=[
                pltpu.VMEM((N, SPAN), BF16),
                pltpu.VMEM((N, width), F32),
                pltpu.VMEM((blocks, per_group, G, 2, entries, SPAN), BF16),
                pltpu.SemaphoreType.DMA((blocks, G)),
                pltpu.SemaphoreType.DMA((blocks, G)),
                pltpu.SemaphoreType.DMA((blocks, per_group)),
                pltpu.SemaphoreType.DMA((blocks, per_group)),
            ],
            compiler_params=pltpu.CompilerParams(
                vmem_limit_bytes=48 * 1024 * 1024,
                dimension_semantics=("arbitrary",),
                collective_id=0,
                has_side_effects=True,
            ),
            cost_estimate=cost,
            name="exchange_forward",
        )(raw, bias, rate, outgoing(b_proj[0], c_proj[0]), x, onehot)
    else:
        bt, ct = gather_rows(b_proj[0], c_proj[0])
        kept = pl.pallas_call(
            forward_kernel,
            grid=(blocks,),
            in_specs=[
                token_rows(lanes, same),
                whole((1, lanes)),
                whole((1, lanes)),
                token_cols(same),
                token_cols(same),
                token_rows(width, same),
                whole((lanes, width)),
            ],
            out_specs=specs,
            out_shape=shapes,
            scratch_shapes=[pltpu.VMEM((N, width), F32)],
            compiler_params=params,
            cost_estimate=cost,
            name="states_forward",
        )(raw, bias, rate, bt, ct, x, onehot)
    ybar, wide_rise, wide_fall, turned_hi, turned_lo, b_rows, step, slope, rise, fall = kept
    at = lambda k: blocks - 1 - k
    grad_x, grad_dt = pl.pallas_call(
        backward_kernel,
        grid=(blocks,),
        in_specs=[token_rows(width, at)] * 5
        + [token_rows(SPAN, at)] * 2
        + [token_rows(N, at), token_cols(at), token_rows(lanes, at), whole((length, lanes))]
        + [token_rows(lanes, at)] * 2
        + [whole((1, lanes)), whole((1, lanes)), whole((lanes, width)), whole((width, lanes))],
        out_specs=[token_rows(width, at), whole((length, heads))],
        out_shape=[
            jax.ShapeDtypeStruct((length, width), BF16),
            jax.ShapeDtypeStruct((length, heads), BF16),
        ],
        scratch_shapes=[pltpu.VMEM((N, width), F32), pltpu.VMEM((length, lanes), F32), pltpu.VMEM((length, lanes), F32)],
        compiler_params=params,
        cost_estimate=pl.CostEstimate(flops=24 * length * N * width, bytes_accessed=20 * length * width, transcendentals=0),
        name="gradients",
    )(
        x, g, ybar, wide_rise, wide_fall, turned_hi, turned_lo, b_rows, ct, step, slope, rise, fall,
        rate, skip, onehot, onehot_t,
    )
    return grad_x[None], grad_dt[None]


def solution(mesh):
    wide, narrow = P("pipe", None, "tp"), P("pipe", "tp")
    return jax.shard_map(
        body,
        mesh=mesh,
        in_specs=(wide, wide, wide, wide, wide, narrow, narrow, narrow),
        out_specs=(wide, wide),
        check_vma=False,
    )
```

```python
import functools

import functools

import jax
import jax.numpy as jnp
import numpy as np
from jax import lax
from jax.experimental import pallas as pl
from jax.experimental.pallas import tpu as pltpu
from jax.sharding import PartitionSpec as P

P_SIZE = 64
N = 256
G = 4
SPAN = 256
COPIES = 3
F32, BF16 = jnp.float32, jnp.bfloat16


def dot(a, b):
    return jnp.dot(a, b, preferred_element_type=F32)


def split2(v):
    hi = v.astype(BF16)
    return hi, (v - hi.astype(F32)).astype(BF16)


def split3(v):
    hi = v.astype(BF16)
    rest = v - hi.astype(F32)
    mid = rest.astype(BF16)
    return hi, mid, (rest - mid.astype(F32)).astype(BF16)


def triangle(lower):
    row = lax.broadcasted_iota(jnp.int32, (SPAN, SPAN), 0)
    col = lax.broadcasted_iota(jnp.int32, (SPAN, SPAN), 1)
    return row >= col if lower else row <= col


def running(mask, v):
    ones = jnp.where(mask, 1.0, 0.0).astype(BF16)
    hi, mid, lo = split3(v)
    return dot(ones, hi) + dot(ones, mid) + dot(ones, lo)


def widen(v, onehot):
    hi, mid, lo = split3(v)
    part = lax.broadcasted_iota(jnp.int32, v.shape, 1) // (v.shape[1] // COPIES)
    parts = jnp.where(part == 0, hi.astype(F32), jnp.where(part == 1, mid.astype(F32), lo.astype(F32)))
    return dot(parts.astype(BF16), onehot)


def head_sum(v, onehot_t):
    hi, lo = split2(v)
    return dot(hi, onehot_t) + dot(lo, onehot_t)


def steps(raw, bias, rate):
    shifted_raw = raw.astype(F32) + bias
    near = jnp.exp(-jnp.abs(shifted_raw))
    step = jnp.maximum(shifted_raw, 0.0) + jnp.log1p(near)
    slope = jnp.where(shifted_raw >= 0, 1.0, near) / (1.0 + near)
    cum = running(triangle(True), rate * step)
    middle = 0.5 * cum[SPAN - 1 :, :]
    return step, slope, jnp.exp(cum - middle), jnp.exp(middle - cum), jnp.exp(middle)


def forward_sends(blocks, per_group, raw, heads_of, out, x, onehot, ct, *rest):
    outs, (bt, state, land, send1, recv1, send2, recv2) = rest[:-7], rest[-7:]
    now = pl.program_id(0)
    me = lax.axis_index("tp")
    group, place = me // per_group, me % per_group

    def across(j, d):
        to = (group + d) % G
        return pltpu.make_async_remote_copy(
            src_ref=out.at[j, to],
            dst_ref=land.at[j, place, group],
            send_sem=send1.at[j, d],
            recv_sem=recv1.at[j, d],
            device_id={"tp": to * per_group + place},
            device_id_type=pl.DeviceIdType.MESH,
        )

    def beside(j, d):
        return pltpu.make_async_remote_copy(
            src_ref=land.at[j, place],
            dst_ref=land.at[j, place],
            send_sem=send2.at[j, d],
            recv_sem=recv2.at[j, d],
            device_id={"tp": group * per_group + (place + d) % per_group},
            device_id_type=pl.DeviceIdType.MESH,
        )

    def own(j):
        return pltpu.make_async_copy(out.at[j, group], land.at[j, place, group], recv1.at[j, 0])

    def pass_on(j):
        own(j).wait()
        for d in range(1, G):
            across(j, d).wait_recv()
        for d in range(1, per_group):
            beside(j, d).start()

    @pl.when(now == 0)
    def _():
        barrier = pltpu.get_barrier_semaphore()
        for d in range(1, G):
            pl.semaphore_signal(
                barrier,
                inc=1,
                device_id={"tp": (group + d) % G * per_group + place},
                device_id_type=pl.DeviceIdType.MESH,
            )
        for d in range(1, per_group):
            pl.semaphore_signal(
                barrier,
                inc=1,
                device_id={"tp": group * per_group + (place + d) % per_group},
                device_id_type=pl.DeviceIdType.MESH,
            )
        pl.semaphore_wait(barrier, G - 1 + per_group - 1)

        @pl.loop(0, blocks)
        def _(j):
            own(j).start()
            for d in range(1, G):
                across(j, d).start()

        pass_on(0)

    @pl.when(now + 1 < blocks)
    def _():
        pass_on(now + 1)

    for d in range(1, per_group):
        beside(now, d).wait_recv()
    bt[...] = land[now, :, :, 0].reshape(N, SPAN)
    ct[...] = land[now, :, :, 1].reshape(N, SPAN)
    forward_kernel(raw, heads_of, bt, ct, x, onehot, *outs, state)

    @pl.when(now == blocks - 1)
    def _():
        @pl.loop(0, blocks)
        def _(j):
            for d in range(1, G):
                across(j, d).wait_send()
            for d in range(1, per_group):
                beside(j, d).wait_send()


def forward_kernel(
    raw, heads_of, bt, ct, x, onehot, ybar, wide_rise, wide_fall, turned_hi, turned_lo, b_out, step_out, slope_out, rise_out, fall_out, state
):
    @pl.when(pl.program_id(0) == 0)
    def _():
        state[...] = jnp.zeros_like(state)

    step, slope, rise, fall, half = steps(raw[...], heads_of[0:1, :], -jnp.exp(heads_of[1:2, :]))
    step_out[...], slope_out[...], rise_out[...], fall_out[...] = step, slope, rise, fall
    wide_rise[...] = widen(rise, onehot[...])
    scale = widen(step * fall, onehot[...])
    wide_fall[...] = scale
    half_row = widen(jnp.broadcast_to(half, (8, half.shape[1])), onehot[...])[0:1]
    x_hi, x_lo = split2(x[...].astype(F32) * scale)
    c_rows, b_rows = ct[...].T, bt[...].T
    b_out[...] = b_rows
    turned_hi[...], turned_lo[...] = split2(jnp.where(triangle(False), dot(b_rows, ct[...]), 0.0))
    s_hi, s_lo = split2(jnp.where(triangle(True), dot(c_rows, bt[...]), 0.0))
    held = half_row * state[...]
    t_hi, t_lo = split2(held)
    ybar[...] = dot(s_hi, x_hi) + dot(s_hi, x_lo) + dot(s_lo, x_hi) + dot(c_rows, t_hi) + dot(c_rows, t_lo)
    state[...] = half_row * (held + dot(bt[...], x_hi) + dot(bt[...], x_lo))


def backward_kernel(
    x, g, ybar, wide_rise, wide_fall, s_hi, s_lo, b_rows, ct, step, slope, rise, fall,
    heads_of, onehot, onehot_t, grad_x, grad_dt, state, by_all, decay_all
):
    now, blocks = pl.program_id(0), pl.num_programs(0)

    @pl.when(now == 0)
    def _():
        state[...] = jnp.zeros_like(state)

    half_row = wide_rise[SPAN - 1 :, :]
    grad = g[...].astype(F32)
    g_hi, g_lo = split2(grad * wide_rise[...])
    held = half_row * state[...]
    t_hi, t_lo = split2(held)
    zbar = dot(s_hi[...], g_hi) + dot(s_hi[...], g_lo) + dot(s_lo[...], g_hi) + dot(b_rows[...], t_hi) + dot(b_rows[...], t_lo)
    state[...] = half_row * (held + dot(ct[...], g_hi) + dot(ct[...], g_lo))
    skip_row = widen(jnp.broadcast_to(heads_of[2:3, :], (8, heads_of.shape[1])), onehot[...])[0:1]
    grad_x[...] = (wide_fall[...] * zbar + skip_row * grad).astype(BF16)
    by_x = fall[...] * head_sum(x[...].astype(F32) * zbar, onehot_t[...])
    by_y = rise[...] * head_sum(grad * ybar[...], onehot_t[...])
    here = pl.ds(pl.multiple_of((blocks - 1 - now) * SPAN, SPAN), SPAN)
    by_all[here, :] = by_x
    decay_all[here, :] = by_y - step[...] * by_x

    @pl.when(now == blocks - 1)
    def _():
        length, heads = grad_dt.shape
        carry = jnp.zeros((1, by_all.shape[1]), F32)
        for j in range(length // SPAN - 1, -1, -1):
            part = slice(j * SPAN, (j + 1) * SPAN)
            decay = running(triangle(False), decay_all[part, :]) + carry
            carry = decay[0:1, :]
            grad_dt[part, :] = (slope[part, :] * (by_all[part, :] - jnp.exp(heads_of[1:2, :]) * decay))[:, :heads].astype(BF16)


def shifted(value, axis, by):
    length = lax.axis_size(axis)
    return lax.ppermute(value, axis, [(i, (i + by) % length) for i in range(length)])


def outgoing(b_proj, c_proj):
    length, columns = b_proj.shape
    width = columns // G
    blocks = length // SPAN
    kind = np.arange(2 * columns) // width % 2
    entry = np.arange(2 * columns) // (2 * width) + np.arange(2 * columns) % width * G
    take = np.arange(columns)[None, :]
    sides = [((entry[:, None] == take) & (kind[:, None] == which)).astype(BF16) for which in range(2)]
    pick = jnp.asarray(np.concatenate(sides, axis=1))
    rows = jnp.concatenate([b_proj, c_proj], axis=1).reshape(blocks, SPAN, 2 * columns)
    turned = jnp.einsum("cd,ktd->kct", pick, rows, preferred_element_type=F32).astype(BF16)
    return turned.reshape(blocks, G, 2, width, SPAN)


def gather_rows(b_proj, c_proj):
    length, columns = b_proj.shape
    ways = lax.axis_size("tp")
    per_group = ways // G
    width = columns // G
    order = (jnp.arange(columns)[:, None] % width) * G + jnp.arange(columns)[:, None] // width
    pick = (order == jnp.arange(columns)[None, :]).astype(BF16)

    def turned(rows):
        return lax.dot_general(pick, rows, (((1,), (1,)), ((), ())), preferred_element_type=F32).astype(BF16)

    both = jnp.stack([turned(b_proj).reshape(G, width, length), turned(c_proj).reshape(G, width, length)], axis=1)
    strided = [[g * per_group + r for g in range(G)] for r in range(per_group)]
    mine = lax.all_to_all(both, "tp", 0, 0, axis_index_groups=strided, tiled=True)
    if per_group > 1:
        close = [[g * per_group + r for r in range(per_group)] for g in range(G)]
        mine = lax.all_gather(mine, "tp", axis=0, axis_index_groups=close, tiled=True)
    return mine[:, 0].reshape(N, length), mine[:, 1].reshape(N, length)


def body(grad_next, inputs, dt_raw, b_proj, c_proj, a_log, dt_bias, skip_gain):
    length, width = inputs.shape[1:]
    heads = a_log.shape[1]
    blocks = length // SPAN
    g = shifted(grad_next[0], "pipe", -1)
    per_group = lax.axis_size("tp") // G
    entries = b_proj.shape[2] // G
    fused = entries % 16 == 0
    raw = jnp.tile(dt_raw[0], (1, COPIES))
    heads_of = jnp.tile(jnp.concatenate([dt_bias, a_log, skip_gain], axis=0), (1, COPIES))
    lanes = heads * COPIES
    onehot = (np.arange(lanes)[:, None] % heads == np.arange(width)[None, :] // P_SIZE).astype(BF16)
    onehot_t = np.ascontiguousarray(onehot.T)
    onehot, onehot_t = jnp.asarray(onehot), jnp.asarray(onehot_t)
    x = inputs[0]

    def whole(shape):
        return pl.BlockSpec(shape, lambda k: (0, 0))

    def token_rows(columns, at):
        return pl.BlockSpec((SPAN, columns), lambda k: (at(k), 0))

    def token_cols(at):
        return pl.BlockSpec((N, SPAN), lambda k: (0, at(k)))

    params = pltpu.CompilerParams(vmem_limit_bytes=62 * 1024 * 1024, dimension_semantics=("arbitrary",))
    same = lambda k: k
    cost = pl.CostEstimate(flops=18 * length * N * width, bytes_accessed=8 * length * width, transcendentals=0)
    specs, shapes = [], []
    for columns, kind in [(width, F32)] * 3 + [(SPAN, BF16)] * 2 + [(N, BF16)] + [(lanes, F32)] * 4:
        specs.append(token_rows(columns, same))
        shapes.append(jax.ShapeDtypeStruct((length, columns), kind))
    if fused:
        ct, *kept = pl.pallas_call(
            functools.partial(forward_sends, blocks, per_group),
            grid=(blocks,),
            in_specs=[
                token_rows(lanes, same),
                whole((3, lanes)),
                pl.BlockSpec(memory_space=pl.ANY),
                token_rows(width, same),
                whole((lanes, width)),
            ],
            out_specs=[token_cols(same)] + specs,
            out_shape=[jax.ShapeDtypeStruct((N, length), BF16)] + shapes,
            scratch_shapes=[
                pltpu.VMEM((N, SPAN), BF16),
                pltpu.VMEM((N, width), F32),
                pltpu.VMEM((blocks, per_group, G, 2, entries, SPAN), BF16),
                pltpu.SemaphoreType.DMA((blocks, G)),
                pltpu.SemaphoreType.DMA((blocks, G)),
                pltpu.SemaphoreType.DMA((blocks, per_group)),
                pltpu.SemaphoreType.DMA((blocks, per_group)),
            ],
            compiler_params=pltpu.CompilerParams(
                vmem_limit_bytes=60 * 1024 * 1024,
                dimension_semantics=("arbitrary",),
                collective_id=0,
                has_side_effects=True,
            ),
            cost_estimate=cost,
            name="exchange_forward",
        )(raw, heads_of, outgoing(b_proj[0], c_proj[0]), x, onehot)
    else:
        bt, ct = gather_rows(b_proj[0], c_proj[0])
        kept = pl.pallas_call(
            forward_kernel,
            grid=(blocks,),
            in_specs=[
                token_rows(lanes, same),
                whole((3, lanes)),
                token_cols(same),
                token_cols(same),
                token_rows(width, same),
                whole((lanes, width)),
            ],
            out_specs=specs,
            out_shape=shapes,
            scratch_shapes=[pltpu.VMEM((N, width), F32)],
            compiler_params=params,
            cost_estimate=cost,
            name="states_forward",
        )(raw, heads_of, bt, ct, x, onehot)
    ybar, wide_rise, wide_fall, turned_hi, turned_lo, b_rows, step, slope, rise, fall = kept
    at = lambda k: blocks - 1 - k
    grad_x, grad_dt = pl.pallas_call(
        backward_kernel,
        grid=(blocks,),
        in_specs=[token_rows(width, at)] * 5
        + [token_rows(SPAN, at)] * 2
        + [token_rows(N, at), token_cols(at), token_rows(lanes, at), whole((length, lanes))]
        + [token_rows(lanes, at)] * 2
        + [whole((3, lanes)), whole((lanes, width)), whole((width, lanes))],
        out_specs=[token_rows(width, at), whole((length, heads))],
        out_shape=[
            jax.ShapeDtypeStruct((length, width), BF16),
            jax.ShapeDtypeStruct((length, heads), BF16),
        ],
        scratch_shapes=[pltpu.VMEM((N, width), F32), pltpu.VMEM((length, lanes), F32), pltpu.VMEM((length, lanes), F32)],
        compiler_params=params,
        cost_estimate=pl.CostEstimate(flops=24 * length * N * width, bytes_accessed=20 * length * width, transcendentals=0),
        name="gradients",
    )(
        x, g, ybar, wide_rise, wide_fall, turned_hi, turned_lo, b_rows, ct, step, slope, rise, fall,
        heads_of, onehot, onehot_t,
    )
    return grad_x[None], grad_dt[None]


def solution(mesh):
    wide, narrow = P("pipe", None, "tp"), P("pipe", "tp")
    return jax.shard_map(
        body,
        mesh=mesh,
        in_specs=(wide, wide, wide, wide, wide, narrow, narrow, narrow),
        out_specs=(wide, wide),
        check_vma=False,
    )
```

```python
import functools

import functools

import jax
import jax.numpy as jnp
import numpy as np
from jax import lax
from jax.experimental import pallas as pl
from jax.experimental.pallas import tpu as pltpu
from jax.sharding import PartitionSpec as P

P_SIZE = 64
N = 256
G = 4
SPAN = 256
COPIES = 3
F32, BF16 = jnp.float32, jnp.bfloat16


def dot(a, b):
    return jnp.dot(a, b, preferred_element_type=F32)


def split2(v):
    hi = v.astype(BF16)
    return hi, (v - hi.astype(F32)).astype(BF16)


def split3(v):
    hi = v.astype(BF16)
    rest = v - hi.astype(F32)
    mid = rest.astype(BF16)
    return hi, mid, (rest - mid.astype(F32)).astype(BF16)


def triangle(lower):
    row = lax.broadcasted_iota(jnp.int32, (SPAN, SPAN), 0)
    col = lax.broadcasted_iota(jnp.int32, (SPAN, SPAN), 1)
    return row >= col if lower else row <= col


def running(mask, v):
    ones = jnp.where(mask, 1.0, 0.0).astype(BF16)
    hi, mid, lo = split3(v)
    return dot(ones, hi) + dot(ones, mid) + dot(ones, lo)


def widen(v, onehot):
    hi, mid, lo = split3(v)
    part = lax.broadcasted_iota(jnp.int32, v.shape, 1) // (v.shape[1] // COPIES)
    parts = jnp.where(part == 0, hi.astype(F32), jnp.where(part == 1, mid.astype(F32), lo.astype(F32)))
    return dot(parts.astype(BF16), onehot)


def head_sum(v, onehot_t):
    hi, lo = split2(v)
    return dot(hi, onehot_t) + dot(lo, onehot_t)


def steps(raw, bias, rate):
    shifted_raw = raw.astype(F32) + bias
    near = jnp.exp(-jnp.abs(shifted_raw))
    step = jnp.maximum(shifted_raw, 0.0) + jnp.log1p(near)
    slope = jnp.where(shifted_raw >= 0, 1.0, near) / (1.0 + near)
    cum = running(triangle(True), rate * step)
    middle = 0.5 * cum[SPAN - 1 :, :]
    return step, slope, jnp.exp(cum - middle), jnp.exp(middle - cum), jnp.exp(middle)


def forward_sends(blocks, per_group, raw, heads_of, out, x, onehot, ct, *rest):
    outs, (bt, state, land, send1, recv1, send2, recv2) = rest[:-7], rest[-7:]
    now = pl.program_id(0)
    me = lax.axis_index("tp")
    group, place = me // per_group, me % per_group

    def across(j, d):
        to = (group + d) % G
        return pltpu.make_async_remote_copy(
            src_ref=out.at[j, to],
            dst_ref=land.at[j, place, group],
            send_sem=send1.at[j, d],
            recv_sem=recv1.at[j, d],
            device_id={"tp": to * per_group + place},
            device_id_type=pl.DeviceIdType.MESH,
        )

    def beside(j, d):
        return pltpu.make_async_remote_copy(
            src_ref=land.at[j, place],
            dst_ref=land.at[j, place],
            send_sem=send2.at[j, d],
            recv_sem=recv2.at[j, d],
            device_id={"tp": group * per_group + (place + d) % per_group},
            device_id_type=pl.DeviceIdType.MESH,
        )

    def own(j):
        return pltpu.make_async_copy(out.at[j, group], land.at[j, place, group], recv1.at[j, 0])

    def pass_on(j):
        own(j).wait()
        for d in range(1, G):
            across(j, d).wait_recv()
        for d in range(1, per_group):
            beside(j, d).start()

    @pl.when(now == 0)
    def _():
        barrier = pltpu.get_barrier_semaphore()
        for d in range(1, G):
            pl.semaphore_signal(
                barrier,
                inc=1,
                device_id={"tp": (group + d) % G * per_group + place},
                device_id_type=pl.DeviceIdType.MESH,
            )
        for d in range(1, per_group):
            pl.semaphore_signal(
                barrier,
                inc=1,
                device_id={"tp": group * per_group + (place + d) % per_group},
                device_id_type=pl.DeviceIdType.MESH,
            )
        pl.semaphore_wait(barrier, G - 1 + per_group - 1)

        @pl.loop(0, blocks)
        def _(j):
            own(j).start()
            for d in range(1, G):
                across(j, d).start()

        pass_on(0)

    @pl.when(now + 1 < blocks)
    def _():
        pass_on(now + 1)

    for d in range(1, per_group):
        beside(now, d).wait_recv()
    bt[...] = land[now, :, :, 0].reshape(N, SPAN)
    ct[...] = land[now, :, :, 1].reshape(N, SPAN)
    forward_kernel(raw, heads_of, bt, ct, x, onehot, *outs, state)

    @pl.when(now == blocks - 1)
    def _():
        @pl.loop(0, blocks)
        def _(j):
            for d in range(1, G):
                across(j, d).wait_send()
            for d in range(1, per_group):
                beside(j, d).wait_send()


def forward_kernel(
    raw, heads_of, bt, ct, x, onehot, ybar, wide_rise, wide_fall, turned_hi, turned_lo, b_out, step_out, slope_out, rise_out, fall_out, state
):
    @pl.when(pl.program_id(0) == 0)
    def _():
        state[...] = jnp.zeros_like(state)

    step, slope, rise, fall, half = steps(raw[...].astype(F32).T, heads_of[0:1, :], -jnp.exp(heads_of[1:2, :]))
    step_out[...], slope_out[...], rise_out[...], fall_out[...] = step, slope, rise, fall
    wide_rise[...] = widen(rise, onehot[...])
    scale = widen(step * fall, onehot[...])
    wide_fall[...] = scale
    half_row = widen(jnp.broadcast_to(half, (8, half.shape[1])), onehot[...])[0:1]
    x_hi, x_lo = split2(x[...].astype(F32) * scale)
    c_rows, b_rows = ct[...].T, bt[...].T
    b_out[...] = b_rows
    turned_hi[...], turned_lo[...] = split2(jnp.where(triangle(False), dot(b_rows, ct[...]), 0.0))
    s_hi, s_lo = split2(jnp.where(triangle(True), dot(c_rows, bt[...]), 0.0))
    held = half_row * state[...]
    t_hi, t_lo = split2(held)
    ybar[...] = dot(s_hi, x_hi) + dot(s_hi, x_lo) + dot(s_lo, x_hi) + dot(c_rows, t_hi) + dot(c_rows, t_lo)
    state[...] = half_row * (held + dot(bt[...], x_hi) + dot(bt[...], x_lo))


def backward_kernel(
    x, g, ybar, wide_rise, wide_fall, s_hi, s_lo, b_rows, ct, step, slope, rise, fall,
    heads_of, onehot, onehot_t, grad_x, grad_dt, state, by_all, decay_all
):
    now, blocks = pl.program_id(0), pl.num_programs(0)

    @pl.when(now == 0)
    def _():
        state[...] = jnp.zeros_like(state)

    half_row = wide_rise[SPAN - 1 :, :]
    grad = g[...].astype(F32)
    g_hi, g_lo = split2(grad * wide_rise[...])
    held = half_row * state[...]
    t_hi, t_lo = split2(held)
    zbar = dot(s_hi[...], g_hi) + dot(s_hi[...], g_lo) + dot(s_lo[...], g_hi) + dot(b_rows[...], t_hi) + dot(b_rows[...], t_lo)
    state[...] = half_row * (held + dot(ct[...], g_hi) + dot(ct[...], g_lo))
    skip_row = widen(jnp.broadcast_to(heads_of[2:3, :], (8, heads_of.shape[1])), onehot[...])[0:1]
    grad_x[...] = (wide_fall[...] * zbar + skip_row * grad).astype(BF16)
    by_x = fall[...] * head_sum(x[...].astype(F32) * zbar, onehot_t[...])
    by_y = rise[...] * head_sum(grad * ybar[...], onehot_t[...])
    here = pl.ds(pl.multiple_of((blocks - 1 - now) * SPAN, SPAN), SPAN)
    by_all[here, :] = by_x
    decay_all[here, :] = by_y - step[...] * by_x

    @pl.when(now == blocks - 1)
    def _():
        heads, length = grad_dt.shape
        carry = jnp.zeros((1, by_all.shape[1]), F32)
        for j in range(length // SPAN - 1, -1, -1):
            part = slice(j * SPAN, (j + 1) * SPAN)
            decay = running(triangle(False), decay_all[part, :]) + carry
            carry = decay[0:1, :]
            turned = (slope[part, :] * (by_all[part, :] - jnp.exp(heads_of[1:2, :]) * decay)).T
            grad_dt[:, part] = turned[:heads].astype(BF16)


def shifted(value, axis, by):
    length = lax.axis_size(axis)
    return lax.ppermute(value, axis, [(i, (i + by) % length) for i in range(length)])


def outgoing(b_proj, c_proj):
    length, columns = b_proj.shape
    width = columns // G
    blocks = length // SPAN
    kind = np.arange(2 * columns) // width % 2
    entry = np.arange(2 * columns) // (2 * width) + np.arange(2 * columns) % width * G
    take = np.arange(columns)[None, :]
    sides = [((entry[:, None] == take) & (kind[:, None] == which)).astype(BF16) for which in range(2)]
    pick = jnp.asarray(np.concatenate(sides, axis=1))
    rows = jnp.concatenate([b_proj, c_proj], axis=1).reshape(blocks, SPAN, 2 * columns)
    turned = jnp.einsum("cd,ktd->kct", pick, rows, preferred_element_type=F32).astype(BF16)
    return turned.reshape(blocks, G, 2, width, SPAN)


def gather_rows(b_proj, c_proj):
    length, columns = b_proj.shape
    ways = lax.axis_size("tp")
    per_group = ways // G
    width = columns // G
    order = (jnp.arange(columns)[:, None] % width) * G + jnp.arange(columns)[:, None] // width
    pick = (order == jnp.arange(columns)[None, :]).astype(BF16)

    def turned(rows):
        return lax.dot_general(pick, rows, (((1,), (1,)), ((), ())), preferred_element_type=F32).astype(BF16)

    both = jnp.stack([turned(b_proj).reshape(G, width, length), turned(c_proj).reshape(G, width, length)], axis=1)
    strided = [[g * per_group + r for g in range(G)] for r in range(per_group)]
    mine = lax.all_to_all(both, "tp", 0, 0, axis_index_groups=strided, tiled=True)
    if per_group > 1:
        close = [[g * per_group + r for r in range(per_group)] for g in range(G)]
        mine = lax.all_gather(mine, "tp", axis=0, axis_index_groups=close, tiled=True)
    return mine[:, 0].reshape(N, length), mine[:, 1].reshape(N, length)


def body(grad_next, inputs, dt_raw, b_proj, c_proj, a_log, dt_bias, skip_gain):
    length, width = inputs.shape[1:]
    heads = a_log.shape[1]
    blocks = length // SPAN
    g = shifted(grad_next[0], "pipe", -1)
    per_group = lax.axis_size("tp") // G
    entries = b_proj.shape[2] // G
    fused = entries % 16 == 0
    raw = jnp.tile(dt_raw[0].T, (COPIES, 1))
    heads_of = jnp.tile(jnp.concatenate([dt_bias, a_log, skip_gain], axis=0), (1, COPIES))
    lanes = heads * COPIES
    onehot = (np.arange(lanes)[:, None] % heads == np.arange(width)[None, :] // P_SIZE).astype(BF16)
    onehot_t = np.ascontiguousarray(onehot.T)
    onehot, onehot_t = jnp.asarray(onehot), jnp.asarray(onehot_t)
    x = inputs[0]

    def whole(shape):
        return pl.BlockSpec(shape, lambda k: (0, 0))

    def token_rows(columns, at):
        return pl.BlockSpec((SPAN, columns), lambda k: (at(k), 0))

    def token_cols(at):
        return pl.BlockSpec((N, SPAN), lambda k: (0, at(k)))

    params = pltpu.CompilerParams(vmem_limit_bytes=62 * 1024 * 1024, dimension_semantics=("arbitrary",))
    same = lambda k: k
    cost = pl.CostEstimate(flops=18 * length * N * width, bytes_accessed=8 * length * width, transcendentals=0)
    specs, shapes = [], []
    for columns, kind in [(width, F32)] * 3 + [(SPAN, BF16)] * 2 + [(N, BF16)] + [(lanes, F32)] * 4:
        specs.append(token_rows(columns, same))
        shapes.append(jax.ShapeDtypeStruct((length, columns), kind))
    if fused:
        ct, *kept = pl.pallas_call(
            functools.partial(forward_sends, blocks, per_group),
            grid=(blocks,),
            in_specs=[
                pl.BlockSpec((lanes, SPAN), lambda k: (0, k)),
                whole((3, lanes)),
                pl.BlockSpec(memory_space=pl.ANY),
                token_rows(width, same),
                whole((lanes, width)),
            ],
            out_specs=[token_cols(same)] + specs,
            out_shape=[jax.ShapeDtypeStruct((N, length), BF16)] + shapes,
            scratch_shapes=[
                pltpu.VMEM((N, SPAN), BF16),
                pltpu.VMEM((N, width), F32),
                pltpu.VMEM((blocks, per_group, G, 2, entries, SPAN), BF16),
                pltpu.SemaphoreType.DMA((blocks, G)),
                pltpu.SemaphoreType.DMA((blocks, G)),
                pltpu.SemaphoreType.DMA((blocks, per_group)),
                pltpu.SemaphoreType.DMA((blocks, per_group)),
            ],
            compiler_params=pltpu.CompilerParams(
                vmem_limit_bytes=60 * 1024 * 1024,
                dimension_semantics=("arbitrary",),
                collective_id=0,
                has_side_effects=True,
            ),
            cost_estimate=cost,
            name="exchange_forward",
        )(raw, heads_of, outgoing(b_proj[0], c_proj[0]), x, onehot)
    else:
        bt, ct = gather_rows(b_proj[0], c_proj[0])
        kept = pl.pallas_call(
            forward_kernel,
            grid=(blocks,),
            in_specs=[
                pl.BlockSpec((lanes, SPAN), lambda k: (0, k)),
                whole((3, lanes)),
                token_cols(same),
                token_cols(same),
                token_rows(width, same),
                whole((lanes, width)),
            ],
            out_specs=specs,
            out_shape=shapes,
            scratch_shapes=[pltpu.VMEM((N, width), F32)],
            compiler_params=params,
            cost_estimate=cost,
            name="states_forward",
        )(raw, heads_of, bt, ct, x, onehot)
    ybar, wide_rise, wide_fall, turned_hi, turned_lo, b_rows, step, slope, rise, fall = kept
    at = lambda k: blocks - 1 - k
    grad_x, grad_dt = pl.pallas_call(
        backward_kernel,
        grid=(blocks,),
        in_specs=[token_rows(width, at)] * 5
        + [token_rows(SPAN, at)] * 2
        + [token_rows(N, at), token_cols(at), token_rows(lanes, at), whole((length, lanes))]
        + [token_rows(lanes, at)] * 2
        + [whole((3, lanes)), whole((lanes, width)), whole((width, lanes))],
        out_specs=[token_rows(width, at), whole((heads, length))],
        out_shape=[
            jax.ShapeDtypeStruct((length, width), BF16),
            jax.ShapeDtypeStruct((heads, length), BF16),
        ],
        scratch_shapes=[pltpu.VMEM((N, width), F32), pltpu.VMEM((length, lanes), F32), pltpu.VMEM((length, lanes), F32)],
        compiler_params=params,
        cost_estimate=pl.CostEstimate(flops=24 * length * N * width, bytes_accessed=20 * length * width, transcendentals=0),
        name="gradients",
    )(
        x, g, ybar, wide_rise, wide_fall, turned_hi, turned_lo, b_rows, ct, step, slope, rise, fall,
        heads_of, onehot, onehot_t,
    )
    return grad_x[None], grad_dt.T[None]


def solution(mesh):
    wide, narrow = P("pipe", None, "tp"), P("pipe", "tp")
    return jax.shard_map(
        body,
        mesh=mesh,
        in_specs=(wide, wide, wide, wide, wide, narrow, narrow, narrow),
        out_specs=(wide, wide),
        check_vma=False,
    )
```
